32 devices in a mesh: dom: 4 (over y, core), fsdp: 8 (over z, x).
Axes of the slice: x: 2, y: 2, z: 4, core: 2. Of those that a mesh axis runs over, the one named last changes fastest.
Arguments:
- features: bfloat16 [128, 1024, 128], P(('dom', 'fsdp')), may hold values from -6 to 6
- history_first: bfloat16 [512, 1024, 128], P('dom', 'fsdp'), may hold values from -6 to 6
- history_second: bfloat16 [512, 1024, 128], P('dom', 'fsdp'), may hold values from -3 to 3
- pull_list: int32 [4, 32, 4], P('dom'), may hold values from 0 to 127
- pull_count: int32 [4, 32], P('dom'), may hold values from 1 to 4, as said below
- tile_src: int32 [128, 6], P(('dom', 'fsdp')), may hold values from 0 to 19
- tile_count: int32 [128], P(('dom', 'fsdp')), may hold values from 1 to 6
- tile_values: bfloat16 [128, 6, 128, 128], P(('dom', 'fsdp')), may hold values from -0.21875 to 0.21875
- w_first: bfloat16 [1024, 1024], P('fsdp'), may hold values from -0.1875 to 0.1875
- w_second: bfloat16 [1024, 1024], P('fsdp'), may hold values from -0.1875 to 0.1875
- bias_first: bfloat16 [1024], P('fsdp'), may hold values from -3 to 3
- out_grad: bfloat16 [128, 1024, 128], P(('dom', 'fsdp')), may hold values from -0.125 to 0.125
Outputs:
- hidden_new: bfloat16 [128, 1024, 128], P(('dom', 'fsdp'))
- grad_w1: float32 [1024, 1024], P('fsdp')
- grad_w2: float32 [1024, 1024], P('fsdp')
- grad_b1: float32 [1024], P('fsdp')
The draws below stay inside these ranges and needn't reach their ends.
Inputs may be any that keep to these rules, and one draw needn't show every extreme that they name: pull_list[o, q, c] numbers a block within partition o. Slot c of list (o, q) is live when c < pull_count[o, q]; every device q has 4 live slots from at least one partition. tile_src below 4 names one of the device's own batch blocks; 4 + s names its pulled slot s.
All inputs are finite; a program needn't handle non-finite values.
Results may differ from the reference program's by a relative error of at most 0.0075.
Values may be sent and summed in bfloat16 or wider, within the bound.
A program may use at most 192 MiB of HBM per device.

```python
import jax
import jax.numpy as jnp
from jax import lax

F = 1024
H = 1024
BLK = 128
TILES = 6
CAP = 4
B_DEV = 4
OWN = 128
PARTITIONS = 4
SOURCES = 20
BATCH_BLK = 128
TABLE_BLK = 512
N_DOM = 4
DEVICES = 32


def draw_pull_count(key, part):
    base_key, full_key = jax.random.split(jax.random.fold_in(key, 7))
    base = jax.random.randint(base_key, (N_DOM, DEVICES), 1, CAP + 1)
    picked = jax.random.randint(full_key, (DEVICES,), 0, N_DOM)
    filled = jnp.arange(N_DOM)[:, None] == picked[None, :]
    return jnp.where(filled, CAP, base).astype(jnp.int32)


def with_ends(array, key, low, top_value):
    spot = [jax.random.randint(jax.random.fold_in(key, axis), (), 0, length) for axis, length in enumerate(array.shape)]
    main_axis = array.shape.index(max(array.shape))
    beside = spot[:main_axis] + [(spot[main_axis] + 1) % array.shape[main_axis]] + spot[main_axis + 1:]
    return array.at[tuple(spot)].set(low).at[tuple(beside)].set(top_value)


def strengthened(values, own_key, source, target, parts, factor):
    owner, partner = [(jnp.arange(values.shape[dim]) // (values.shape[dim] // parts)).reshape([-1 if axis == dim else 1 for axis in range(values.ndim)]) for dim in (source, target)]
    chosen = jax.random.permutation(own_key, parts)[partner]
    strong = (owner == chosen) | (owner == (partner + parts // 2) % parts)
    return jnp.where(strong, factor * values, values)


def steps_of(key, dims, cuts, least, largest):
    gain = 1.0
    for dim, shards_of in cuts:
        steps = jax.random.uniform(jax.random.fold_in(jax.random.fold_in(key, 6), dim), (shards_of,), jnp.float32, least / len(cuts), largest / len(cuts))
        gain = gain * jnp.repeat(jnp.exp(steps), dims[dim] // shards_of).reshape((-1,) + (1,) * (len(dims) - 1 - dim))
    return gain


def scatter_about(stream_key, dims, spread, limit, cuts=(), kind=jnp.bfloat16):
    values = spread * jax.random.normal(stream_key, dims, jnp.float32)
    if cuts:
        values = values * steps_of(stream_key, dims, cuts, -0.22, 0.18)
    return jnp.clip(values, -limit, limit).astype(kind)


def gaussian_with(key, extent, width, limit, shards, heavy, held_as=jnp.bfloat16):
    entries = width * jax.random.normal(key, extent, jnp.float32)
    if shards:
        entries = entries * steps_of(key, extent, shards, -0.22, 0.18)
    return jnp.clip(strengthened(entries, jax.random.fold_in(key, 3), *heavy), -limit, limit).astype(held_as)


def setup_inputs(seed: int = 0) -> dict:
    keys = jax.random.split(jax.random.key(seed), 13)
    features = gaussian_with(keys[0], (BATCH_BLK, F, BLK), 1.0, 6.0, ((0, 32),), (0, 1, 32, 2.75))
    history_first = scatter_about(keys[1], (TABLE_BLK, F, BLK), 1.0, 6.0, ((0, 4), (1, 8)))
    history_second = scatter_about(keys[2], (TABLE_BLK, H, BLK), 0.5, 3.0, ((0, 4), (1, 8)))
    pull_list = with_ends(jax.random.randint(keys[3], (PARTITIONS, DEVICES, CAP), 0, OWN), jax.random.fold_in(keys[3], 1), 0, OWN - 1).astype(jnp.int32)
    pull_count = draw_pull_count(jax.random.fold_in(keys[12], 71), 0)
    tile_src = with_ends(jax.random.randint(keys[5], (BATCH_BLK, TILES), 0, SOURCES), jax.random.fold_in(keys[5], 1), 0, SOURCES - 1).astype(jnp.int32)
    tile_count = with_ends(jax.random.randint(keys[6], (BATCH_BLK,), 1, TILES + 1), jax.random.fold_in(keys[6], 1), 1, TILES).astype(jnp.int32)
    tile_values = scatter_about(keys[7], (BATCH_BLK, TILES, BLK, BLK), (BLK * TILES) ** -0.5, 0.21875, ((0, 32),))
    w_first = scatter_about(keys[8], (F, H), F ** -0.5, 0.1875, ((0, 8),))
    w_second = scatter_about(keys[9], (H, H), H ** -0.5, 0.1875, ((0, 8),))
    bias_first = scatter_about(keys[10], (H,), 0.5, 3.0, ((0, 8),))
    out_grad = scatter_about(keys[11], (BATCH_BLK, H, BLK), ((BATCH_BLK * BLK) ** -0.5), 0.125, ((0, 32),))
    return dict(features=features, history_first=history_first, history_second=history_second, pull_list=pull_list, pull_count=pull_count, tile_src=tile_src, tile_count=tile_count, tile_values=tile_values, w_first=w_first, w_second=w_second, bias_first=bias_first, out_grad=out_grad)


def gelu_tanh(inputs):
    return jax.nn.gelu(inputs, approximate=True)

def aggregate(sources, source_ids, tile_live, tile_vals):
    running = jnp.zeros((source_ids.shape[0], sources.shape[1], sources.shape[2]), jnp.float32)
    for tile_slot in range(TILES):
        blocks = jnp.take(sources, source_ids[:, tile_slot], axis=0).astype(jnp.float32)
        product = jnp.einsum('vfj,vji->vfi', blocks, tile_vals[:, tile_slot].astype(jnp.float32))
        running = running + jnp.where(tile_live[:, tile_slot][:, None, None], product, 0.0)
    return running

def spread_back(back_second, source_ids, tile_live, tile_vals):
    targets = jnp.arange(B_DEV, dtype=jnp.int32)[None, :]
    running = jnp.zeros(back_second.shape, jnp.float32)
    for tile_slot in range(TILES):
        product = jnp.einsum('vai,vji->vaj', back_second.astype(jnp.float32), tile_vals[:, tile_slot].astype(jnp.float32))
        matches = jnp.where((source_ids[:, tile_slot][:, None] == targets) & tile_live[:, tile_slot][:, None], 1.0, 0.0).astype(jnp.float32)
        running = running + jnp.einsum('vu,vaj->uaj', matches, product, precision=lax.Precision.HIGHEST)
    return running

def reference(features, history_first, history_second, pull_list, pull_count, tile_src, tile_count, tile_values, w_first, w_second, bias_first, out_grad):
    owners = jnp.arange(PARTITIONS, dtype=jnp.int32)
    first_weight = w_first.astype(jnp.float32)
    second_weight = w_second.astype(jnp.float32)
    bias_full = bias_first.astype(jnp.float32)

    def per_device(sums_so_far, device):
        first_sum, second_sum, bias_sum = sums_so_far
        first_block = (device * B_DEV).astype(jnp.int32)
        own_feats = lax.dynamic_slice_in_dim(features, first_block, B_DEV, 0)
        source_ids = lax.dynamic_slice_in_dim(tile_src, first_block, B_DEV, 0)
        live_tiles = lax.dynamic_slice_in_dim(tile_count, first_block, B_DEV, 0)
        tile_vals = lax.dynamic_slice_in_dim(tile_values, first_block, B_DEV, 0)
        cotangent = lax.dynamic_slice_in_dim(out_grad, first_block, B_DEV, 0)
        chosen = lax.dynamic_index_in_dim(pull_list, device, 1, keepdims=False)
        live_count = lax.dynamic_index_in_dim(pull_count, device, 1, keepdims=False)
        block_rows = (chosen + OWN * owners[:, None]).T.reshape(-1).astype(jnp.int32)
        is_live = (jnp.arange(CAP, dtype=jnp.int32)[None, :] < live_count[:, None]).T.reshape(-1)
        pulled_first = jnp.where(is_live[:, None, None], jnp.take(history_first, block_rows, axis=0), jnp.zeros((), history_first.dtype))
        pulled_second = jnp.where(is_live[:, None, None], jnp.take(history_second, block_rows, axis=0), jnp.zeros((), history_second.dtype))
        tile_live = jnp.arange(TILES, dtype=jnp.int32)[None, :] < live_tiles[:, None]
        agg_first = aggregate(jnp.concatenate([own_feats, pulled_first], 0), source_ids, tile_live, tile_vals).astype(jnp.bfloat16)
        pre_act = jnp.einsum('fh,vfn->vhn', first_weight, agg_first.astype(jnp.float32)) + bias_full[None, :, None]
        hidden_out = gelu_tanh(pre_act).astype(jnp.bfloat16)
        agg_second = aggregate(jnp.concatenate([hidden_out, pulled_second], 0), source_ids, tile_live, tile_vals).astype(jnp.bfloat16)
        second_term = jnp.einsum('van,vbn->ab', agg_second.astype(jnp.float32), cotangent.astype(jnp.float32))
        back_second = jnp.einsum('ab,vbn->van', second_weight, cotangent.astype(jnp.float32)).astype(jnp.bfloat16)
        back_hidden = spread_back(back_second, source_ids, tile_live, tile_vals)
        _, pullback = jax.vjp(gelu_tanh, pre_act)
        back_pre = pullback(back_hidden)[0].astype(jnp.bfloat16)
        first_term = jnp.einsum('vfn,vhn->fh', agg_first.astype(jnp.float32), back_pre.astype(jnp.float32))
        bias_term = lax.optimization_barrier(jnp.sum(back_pre.astype(jnp.float32), axis=(0, 2)))
        return ((first_sum + first_term, second_sum + second_term, bias_sum + bias_term), hidden_out)
    zero_sums = (jnp.zeros((F, H), jnp.float32), jnp.zeros((H, H), jnp.float32), jnp.zeros((H,), jnp.float32))
    totals, hidden_all = lax.scan(per_device, zero_sums, jnp.arange(DEVICES, dtype=jnp.int32))
    return (hidden_all.reshape(BATCH_BLK, H, BLK), totals[0], totals[1], totals[2])
```

```python
import functools

import jax
import jax.numpy as jnp
from jax import lax
from jax.experimental import pallas as pl
from jax.experimental.pallas import tpu as pltpu
from jax.sharding import PartitionSpec as P

F32 = jnp.float32
BF16 = jnp.bfloat16
CHUNK = 256
VMEM_BYTES = 48 * 1024 * 1024
LAST = (((1,), (1,)), ((), ()))


def add_sources(v, src_ref, cnt_ref, own_ref, arr_ref, tiles_ref, acc):
    own_count = own_ref.shape[0]
    parts = arr_ref.shape[0]
    acc[...] = jnp.zeros_like(acc)

    def step(t, carry):
        source = src_ref[v, t]
        tile = tiles_ref[v, t]

        @pl.when(source < own_count)
        def _():
            acc[...] += jnp.dot(own_ref[source], tile, preferred_element_type=F32)

        @pl.when(source >= own_count)
        def _():
            slot = source - own_count
            block = arr_ref[lax.rem(slot, parts), :, lax.div(slot, parts)]
            block = block.reshape(acc.shape)
            acc[...] += jnp.dot(block, tile, preferred_element_type=F32)

        return carry

    lax.fori_loop(0, cnt_ref[v], step, 0)


def outer_kernel_loop(left, right, out_ref):
    @pl.loop(0, left.shape[0] // CHUNK)
    def _(r):
        rows = pl.ds(pl.multiple_of(r * CHUNK, CHUNK), CHUNK)
        out_ref[rows, :] = lax.dot_general(
            left[rows, :], right[...], LAST, preferred_element_type=F32
        )


def back_kernel(src_ref, cnt_ref, w_ref, grad_ref, tiles_ref, out_ref, wide, second):
    count, _, block = grad_ref.shape
    for v in range(count):
        wide[:, v * block : (v + 1) * block] = grad_ref[v]

    @pl.loop(0, w_ref.shape[0] // CHUNK)
    def _(r):
        rows = pl.ds(pl.multiple_of(r * CHUNK, CHUNK), CHUNK)
        product = jnp.dot(w_ref[rows, :], wide[...], preferred_element_type=F32).astype(BF16)
        for v in range(count):
            second[v, rows, :] = product[:, v * block : (v + 1) * block]

    out_ref[...] = jnp.zeros_like(out_ref)
    for v in range(count):

        def step(t, carry, v=v):
            source = src_ref[v, t]

            @pl.when(source < count)
            def _():
                out_ref[source] += lax.dot_general(
                    second[v], tiles_ref[v, t], LAST, preferred_element_type=F32
                )

            return carry

        lax.fori_loop(0, cnt_ref[v], step, 0)


def first_kernel(
    src_ref, cnt_ref, own_ref, arr_ref, tiles_ref, w_ref, bias_ref, back_ref,
    hidden_ref, grad_ref, sum_ref, acc, agg, pre_grad,
):
    count, _, block = own_ref.shape
    for v in range(count):
        add_sources(v, src_ref, cnt_ref, own_ref, arr_ref, tiles_ref, acc)
        agg[:, v * block : (v + 1) * block] = acc[...].astype(BF16)

    @pl.loop(0, w_ref.shape[0] // CHUNK)
    def _(r):
        rows = pl.ds(pl.multiple_of(r * CHUNK, CHUNK), CHUNK)
        x = jnp.dot(w_ref[rows, :], agg[...], preferred_element_type=F32) + bias_ref[rows, :]
        square = x * x
        bent = jnp.tanh(0.7978845608028654 * x * (1.0 + 0.044715 * square))
        half = 0.5 + 0.5 * bent
        hidden = (x * half).astype(BF16)
        slope = half + 0.5 * x * (1.0 - bent * bent) * (
            0.7978845608028654 * (1.0 + 3.0 * 0.044715 * square)
        )
        for v in range(count):
            columns = slice(v * block, (v + 1) * block)
            hidden_ref[v, rows, :] = hidden[:, columns]
            pre_grad[rows, columns] = (back_ref[v, rows, :] * slope[:, columns]).astype(BF16)

    outer_kernel_loop(agg, pre_grad, grad_ref)
    ones = jnp.ones((sum_ref.shape[0], pre_grad.shape[1]), BF16)
    sum_ref[...] = lax.dot_general(ones, pre_grad[...], LAST, preferred_element_type=F32)


def second_kernel(
    src_ref, cnt_ref, own_ref, arr_ref, tiles_ref, cot_ref, grad_ref, acc, agg, wide
):
    count, _, block = own_ref.shape
    for v in range(count):
        add_sources(v, src_ref, cnt_ref, own_ref, arr_ref, tiles_ref, acc)
        agg[:, v * block : (v + 1) * block] = acc[...].astype(BF16)
        wide[:, v * block : (v + 1) * block] = cot_ref[v]
    outer_kernel_loop(agg, wide, grad_ref)


def local_call(kernel, name, scalars, operands, out_shape, scratch, flops):
    in_specs = [pl.BlockSpec(memory_space=pltpu.SMEM)] * len(scalars)
    in_specs += [pl.BlockSpec(memory_space=pltpu.VMEM)] * len(operands)
    moved = sum(a.size * a.dtype.itemsize for a in operands)
    return pl.pallas_call(
        kernel,
        name=name,
        out_shape=out_shape,
        in_specs=in_specs,
        out_specs=jax.tree.map(lambda _: pl.BlockSpec(memory_space=pltpu.VMEM), out_shape),
        scratch_shapes=scratch,
        compiler_params=pltpu.CompilerParams(vmem_limit_bytes=VMEM_BYTES),
        cost_estimate=pl.CostEstimate(flops=flops, bytes_accessed=moved * 2, transcendentals=0),
    )(*scalars, *operands)


def shifted(axis_name, size, stride, length, k):
    pairs = []
    for index in range(size):
        digit = index // stride % length
        pairs.append((index, index + ((digit + k) % length - digit) * stride))
    return functools.partial(lax.ppermute, axis_name=axis_name, perm=pairs)


def scatter_sum(terms, dim, hop, digit, length):
    mine = lax.dynamic_index_in_dim(terms, digit, dim, keepdims=False)
    for k in range(1, length):
        theirs = lax.dynamic_index_in_dim(terms, (digit + k) % length, dim, keepdims=False)
        mine = mine + hop(k)(theirs.astype(BF16)).astype(F32)
    return mine


def gather_all(piece, hop, digit, length):
    whole = jnp.zeros((length,) + piece.shape, piece.dtype)
    whole = lax.dynamic_update_index_in_dim(whole, piece, digit, 0)
    for k in range(1, length):
        whole = lax.dynamic_update_index_in_dim(
            whole, hop(k)(piece), (digit - k + length) % length, 0
        )
    return whole


def sum_all(vector, hop, length):
    total = vector
    for k in range(1, length):
        total = total + hop(k)(vector)
    return total


def on_device(
    features,
    history_first,
    history_second,
    pull_list,
    pull_count,
    tile_src,
    tile_count,
    tile_values,
    w_first,
    w_second,
    bias_first,
    out_grad,
):
    dom_size = lax.axis_size("dom")
    fsdp_size = lax.axis_size("fsdp")
    dom_index = lax.axis_index("dom")
    fsdp_index = lax.axis_index("fsdp")
    cores = 2 if dom_size % 2 == 0 else 1
    y_size = dom_size // cores
    z_size = 4 if fsdp_size % 4 == 0 else 1
    x_size = fsdp_size // z_size
    core, y = dom_index % cores, dom_index // cores
    x, z = fsdp_index % x_size, fsdp_index // x_size

    def core_hop(k):
        return shifted("dom", dom_size, 1, cores, k)

    def y_hop(k):
        return shifted("dom", dom_size, cores, y_size, k)

    def x_hop(k):
        return shifted("fsdp", fsdp_size, 1, x_size, k)

    def z_hop(k):
        return shifted("fsdp", fsdp_size, x_size, z_size, k)

    count, width, block = features.shape
    hidden_width = w_first.shape[1]

    chosen = pull_list[0]
    requesters, cap = chosen.shape
    live = lax.broadcasted_iota(jnp.int32, chosen.shape, 1) < pull_count[0][:, None]

    def pull(table):
        taken = jnp.take(table, chosen.reshape(-1), axis=0)
        taken = taken.reshape(chosen.shape + table.shape[1:])
        sent = jnp.where(live[:, :, None, None], taken, jnp.zeros((), table.dtype))
        got = lax.all_to_all(sent, ("dom", "fsdp"), split_axis=0, concat_axis=0, tiled=True)
        return got.reshape(dom_size, fsdp_size, cap, table.shape[1], block)

    arrived_first = pull(history_first)
    arrived_second = pull(history_second)

    rows = w_first.shape[0]
    share = rows // dom_size
    bias_row = jnp.pad(bias_first[None, :], ((0, 15), (0, hidden_width - bias_first.shape[0])))
    payload = jnp.concatenate(
        [
            lax.dynamic_slice_in_dim(w_first, dom_index * share, share, 0),
            lax.dynamic_slice_in_dim(w_second, dom_index * share, share, 0),
            bias_row,
        ],
        0,
    )
    along = lax.all_gather(payload, "fsdp", axis=0)
    bias_full = along[:, 2 * share, : bias_first.shape[0]].reshape(hidden_width)
    both = lax.all_gather(along[:, : 2 * share], "dom", axis=0)
    both = both.reshape(dom_size, fsdp_size, 2, share, hidden_width)
    both = both.transpose(2, 1, 0, 3, 4).reshape(2, width, hidden_width)
    first_turned = both[0].T
    second_full = both[1]

    scalars = (tile_src, tile_count)
    wide = count * block
    mat = 2 * width * hidden_width * wide
    back_hidden = local_call(
        back_kernel,
        "back_to_hidden",
        scalars,
        (second_full, out_grad, tile_values),
        jax.ShapeDtypeStruct((count, hidden_width, block), F32),
        [
            pltpu.VMEM((hidden_width, wide), BF16),
            pltpu.VMEM((count, hidden_width, block), BF16),
        ],
        2 * mat,
    )
    hidden_new, first_term, bias_rows = local_call(
        first_kernel,
        "first_layer",
        scalars,
        (
            features,
            arrived_first,
            tile_values,
            first_turned,
            bias_full.astype(F32)[:, None],
            back_hidden,
        ),
        (
            jax.ShapeDtypeStruct((count, hidden_width, block), BF16),
            jax.ShapeDtypeStruct((width, hidden_width), F32),
            jax.ShapeDtypeStruct((8, hidden_width), F32),
        ),
        [
            pltpu.VMEM((width, block), F32),
            pltpu.VMEM((width, wide), BF16),
            pltpu.VMEM((hidden_width, wide), BF16),
        ],
        4 * mat,
    )
    second_term = local_call(
        second_kernel,
        "second_layer",
        scalars,
        (hidden_new, arrived_second, tile_values, out_grad),
        jax.ShapeDtypeStruct((hidden_width, hidden_width), F32),
        [
            pltpu.VMEM((hidden_width, block), F32),
            pltpu.VMEM((hidden_width, wide), BF16),
            pltpu.VMEM((hidden_width, wide), BF16),
        ],
        3 * mat,
    )

    def total(term):
        terms = term.reshape(z_size, x_size, y_size, cores, share, hidden_width)
        terms = scatter_sum(terms, 3, core_hop, core, cores)
        terms = scatter_sum(terms, 1, x_hop, x, x_size)
        terms = scatter_sum(terms, 1, y_hop, y, y_size)
        piece = scatter_sum(terms, 0, z_hop, z, z_size)
        pieces = gather_all(piece, y_hop, y, y_size)
        pieces = gather_all(pieces, core_hop, core, cores)
        return pieces.transpose(1, 0, 2, 3).reshape(rows, hidden_width)

    bias_sum = sum_all(bias_rows[0], core_hop, cores)
    bias_sum = sum_all(bias_sum, x_hop, x_size)
    bias_sum = sum_all(bias_sum, y_hop, y_size)
    bias_sum = sum_all(bias_sum, z_hop, z_size)
    bias_len = bias_first.shape[0]
    bias_total = lax.dynamic_slice_in_dim(bias_sum, fsdp_index * bias_len, bias_len, 0)
    return (hidden_new, total(first_term), total(second_term), bias_total)


def solution(mesh):
    return jax.shard_map(
        on_device,
        mesh=mesh,
        in_specs=(
            P(("dom", "fsdp"), None, None),
            P("dom", "fsdp", None),
            P("dom", "fsdp", None),
            P("dom", None, None),
            P("dom", None),
            P(("dom", "fsdp"), None),
            P(("dom", "fsdp")),
            P(("dom", "fsdp"), None, None, None),
            P("fsdp", None),
            P("fsdp", None),
            P("fsdp"),
            P(("dom", "fsdp"), None, None),
        ),
        out_specs=(P(("dom", "fsdp"), None, None), P("fsdp", None), P("fsdp", None), P("fsdp")),
        check_vma=False,
    )
```

```python
import functools

import jax
import jax.numpy as jnp
from jax import lax
from jax.experimental import pallas as pl
from jax.experimental.pallas import tpu as pltpu
from jax.sharding import PartitionSpec as P

F32 = jnp.float32
BF16 = jnp.bfloat16
CHUNK = 256
VMEM_BYTES = 48 * 1024 * 1024
LAST = (((1,), (1,)), ((), ()))


def add_sources(v, src_ref, cnt_ref, own_ref, arr_ref, tiles_ref, acc):
    own_count = own_ref.shape[0]
    parts = arr_ref.shape[0]
    acc[...] = jnp.zeros_like(acc)

    def step(t, carry):
        source = src_ref[v, t]
        tile = tiles_ref[v, t]

        @pl.when(source < own_count)
        def _():
            acc[...] += jnp.dot(own_ref[source], tile, preferred_element_type=F32)

        @pl.when(source >= own_count)
        def _():
            slot = source - own_count
            block = arr_ref[lax.rem(slot, parts), :, lax.div(slot, parts)]
            block = block.reshape(acc.shape)
            acc[...] += jnp.dot(block, tile, preferred_element_type=F32)

        return carry

    lax.fori_loop(0, cnt_ref[v], step, 0)


def outer_kernel_loop(left, right, out_ref):
    @pl.loop(0, left.shape[0] // CHUNK)
    def _(r):
        rows = pl.ds(pl.multiple_of(r * CHUNK, CHUNK), CHUNK)
        out_ref[rows, :] = lax.dot_general(
            left[rows, :], right[...], LAST, preferred_element_type=F32
        )


def back_kernel(src_ref, cnt_ref, w_ref, grad_ref, tiles_ref, out_ref, wide, second):
    count, _, block = grad_ref.shape
    for v in range(count):
        wide[:, v * block : (v + 1) * block] = grad_ref[v]

    @pl.loop(0, w_ref.shape[0] // CHUNK)
    def _(r):
        rows = pl.ds(pl.multiple_of(r * CHUNK, CHUNK), CHUNK)
        product = jnp.dot(w_ref[rows, :], wide[...], preferred_element_type=F32).astype(BF16)
        for v in range(count):
            second[v, rows, :] = product[:, v * block : (v + 1) * block]

    out_ref[...] = jnp.zeros_like(out_ref)
    for v in range(count):

        def step(t, carry, v=v):
            source = src_ref[v, t]

            @pl.when(source < count)
            def _():
                out_ref[source] += lax.dot_general(
                    second[v], tiles_ref[v, t], LAST, preferred_element_type=F32
                )

            return carry

        lax.fori_loop(0, cnt_ref[v], step, 0)


def first_kernel(
    src_ref, cnt_ref, own_ref, arr_ref, tiles_ref, w_ref, bias_ref, back_ref,
    hidden_ref, grad_ref, sum_ref, acc, agg, pre_grad,
):
    count, _, block = own_ref.shape
    for v in range(count):
        add_sources(v, src_ref, cnt_ref, own_ref, arr_ref, tiles_ref, acc)
        agg[:, v * block : (v + 1) * block] = acc[...].astype(BF16)

    @pl.loop(0, w_ref.shape[0] // CHUNK)
    def _(r):
        rows = pl.ds(pl.multiple_of(r * CHUNK, CHUNK), CHUNK)
        x = jnp.dot(w_ref[rows, :], agg[...], preferred_element_type=F32) + bias_ref[rows, :]
        square = x * x
        bent = jnp.tanh(0.7978845608028654 * x * (1.0 + 0.044715 * square))
        half = 0.5 + 0.5 * bent
        hidden = (x * half).astype(BF16)
        slope = half + 0.5 * x * (1.0 - bent * bent) * (
            0.7978845608028654 * (1.0 + 3.0 * 0.044715 * square)
        )
        for v in range(count):
            columns = slice(v * block, (v + 1) * block)
            hidden_ref[v, rows, :] = hidden[:, columns]
            pre_grad[rows, columns] = (back_ref[v, rows, :] * slope[:, columns]).astype(BF16)

    outer_kernel_loop(agg, pre_grad, grad_ref)
    ones = jnp.ones((sum_ref.shape[0], pre_grad.shape[1]), BF16)
    sum_ref[...] = lax.dot_general(ones, pre_grad[...], LAST, preferred_element_type=F32)


def second_kernel(
    src_ref, cnt_ref, own_ref, arr_ref, tiles_ref, cot_ref, grad_ref, acc, agg, wide
):
    count, _, block = own_ref.shape
    for v in range(count):
        add_sources(v, src_ref, cnt_ref, own_ref, arr_ref, tiles_ref, acc)
        agg[:, v * block : (v + 1) * block] = acc[...].astype(BF16)
        wide[:, v * block : (v + 1) * block] = cot_ref[v]
    outer_kernel_loop(agg, wide, grad_ref)


def local_call(kernel, name, scalars, operands, out_shape, scratch, flops):
    in_specs = [pl.BlockSpec(memory_space=pltpu.SMEM)] * len(scalars)
    in_specs += [pl.BlockSpec(memory_space=pltpu.VMEM)] * len(operands)
    moved = sum(a.size * a.dtype.itemsize for a in operands)
    return pl.pallas_call(
        kernel,
        name=name,
        out_shape=out_shape,
        in_specs=in_specs,
        out_specs=jax.tree.map(lambda _: pl.BlockSpec(memory_space=pltpu.VMEM), out_shape),
        scratch_shapes=scratch,
        compiler_params=pltpu.CompilerParams(vmem_limit_bytes=VMEM_BYTES),
        cost_estimate=pl.CostEstimate(flops=flops, bytes_accessed=moved * 2, transcendentals=0),
    )(*scalars, *operands)


def shifted(axis_name, size, stride, length, k):
    pairs = []
    for index in range(size):
        digit = index // stride % length
        pairs.append((index, index + ((digit + k) % length - digit) * stride))
    return functools.partial(lax.ppermute, axis_name=axis_name, perm=pairs)


def scatter_sum(terms, dim, hop, digit, length):
    mine = lax.dynamic_index_in_dim(terms, digit, dim, keepdims=False)
    for k in range(1, length):
        theirs = lax.dynamic_index_in_dim(terms, (digit + k) % length, dim, keepdims=False)
        mine = mine + hop(k)(theirs.astype(BF16)).astype(F32)
    return mine


def gather_all(piece, hop, digit, length):
    whole = jnp.zeros((length,) + piece.shape, piece.dtype)
    whole = lax.dynamic_update_index_in_dim(whole, piece, digit, 0)
    for k in range(1, length):
        whole = lax.dynamic_update_index_in_dim(
            whole, hop(k)(piece), (digit - k + length) % length, 0
        )
    return whole


def sum_all(vector, hop, length):
    total = vector
    for k in range(1, length):
        total = total + hop(k)(vector)
    return total


def on_device(
    features,
    history_first,
    history_second,
    pull_list,
    pull_count,
    tile_src,
    tile_count,
    tile_values,
    w_first,
    w_second,
    bias_first,
    out_grad,
):
    dom_size = lax.axis_size("dom")
    fsdp_size = lax.axis_size("fsdp")
    dom_index = lax.axis_index("dom")
    fsdp_index = lax.axis_index("fsdp")
    cores = 2 if dom_size % 2 == 0 else 1
    y_size = dom_size // cores
    z_size = 4 if fsdp_size % 4 == 0 else 1
    x_size = fsdp_size // z_size
    core, y = dom_index % cores, dom_index // cores
    x, z = fsdp_index % x_size, fsdp_index // x_size

    def core_hop(k):
        return shifted("dom", dom_size, 1, cores, k)

    def y_hop(k):
        return shifted("dom", dom_size, cores, y_size, k)

    def x_hop(k):
        return shifted("fsdp", fsdp_size, 1, x_size, k)

    def z_hop(k):
        return shifted("fsdp", fsdp_size, x_size, z_size, k)

    count, width, block = features.shape
    hidden_width = w_first.shape[1]

    chosen = pull_list[0]
    requesters, cap = chosen.shape
    live = lax.broadcasted_iota(jnp.int32, chosen.shape, 1) < pull_count[0][:, None]

    def picked(table):
        taken = jnp.take(table, chosen.reshape(-1), axis=0)
        taken = taken.reshape(chosen.shape + table.shape[1:])
        return jnp.where(live[:, :, None, None], taken, jnp.zeros((), table.dtype))

    def pull(sent):
        got = lax.all_to_all(sent, ("dom", "fsdp"), split_axis=0, concat_axis=0, tiled=True)
        return got.reshape(dom_size, fsdp_size, cap, sent.shape[2], block)

    rows = w_first.shape[0]
    share = rows // dom_size
    bias_row = jnp.pad(bias_first[None, :], ((0, 15), (0, hidden_width - bias_first.shape[0])))
    payload = jnp.concatenate(
        [
            lax.dynamic_slice_in_dim(w_first, dom_index * share, share, 0),
            lax.dynamic_slice_in_dim(w_second, dom_index * share, share, 0),
            bias_row,
        ],
        0,
    )
    along = lax.all_gather(payload, "fsdp", axis=0)
    sent_first, sent_second, along = lax.optimization_barrier(
        (picked(history_first), picked(history_second), along)
    )
    arrived_first = pull(sent_first)
    bias_full = along[:, 2 * share, : bias_first.shape[0]].reshape(hidden_width)
    both = lax.all_gather(along[:, : 2 * share], "dom", axis=0)
    both = both.reshape(dom_size, fsdp_size, 2, share, hidden_width)
    both = both.transpose(2, 1, 0, 3, 4).reshape(2, width, hidden_width)
    first_turned = both[0].T
    second_full = both[1]

    scalars = (tile_src, tile_count)
    wide = count * block
    mat = 2 * width * hidden_width * wide
    back_hidden = local_call(
        back_kernel,
        "back_to_hidden",
        scalars,
        (second_full, out_grad, tile_values),
        jax.ShapeDtypeStruct((count, hidden_width, block), F32),
        [
            pltpu.VMEM((hidden_width, wide), BF16),
            pltpu.VMEM((count, hidden_width, block), BF16),
        ],
        2 * mat,
    )
    sent_second, arrived_first, first_turned, back_hidden = lax.optimization_barrier(
        (sent_second, arrived_first, first_turned, back_hidden)
    )
    arrived_second = pull(sent_second)
    hidden_new, first_term, bias_rows = local_call(
        first_kernel,
        "first_layer",
        scalars,
        (
            features,
            arrived_first,
            tile_values,
            first_turned,
            bias_full.astype(F32)[:, None],
            back_hidden,
        ),
        (
            jax.ShapeDtypeStruct((count, hidden_width, block), BF16),
            jax.ShapeDtypeStruct((width, hidden_width), F32),
            jax.ShapeDtypeStruct((8, hidden_width), F32),
        ),
        [
            pltpu.VMEM((width, block), F32),
            pltpu.VMEM((width, wide), BF16),
            pltpu.VMEM((hidden_width, wide), BF16),
        ],
        4 * mat,
    )
    def near_sum(term):
        terms = term.reshape(z_size, x_size, y_size, cores, share, hidden_width)
        terms = scatter_sum(terms, 3, core_hop, core, cores)
        terms = scatter_sum(terms, 1, x_hop, x, x_size)
        return scatter_sum(terms, 1, y_hop, y, y_size)

    first_near = near_sum(first_term)
    bias_sum = sum_all(bias_rows[0], core_hop, cores)
    bias_sum = sum_all(bias_sum, x_hop, x_size)
    bias_sum = sum_all(bias_sum, y_hop, y_size)
    hidden_held, arrived_second, first_near, bias_sum = lax.optimization_barrier(
        (hidden_new, arrived_second, first_near, bias_sum)
    )
    second_term = local_call(
        second_kernel,
        "second_layer",
        scalars,
        (hidden_held, arrived_second, tile_values, out_grad),
        jax.ShapeDtypeStruct((hidden_width, hidden_width), F32),
        [
            pltpu.VMEM((hidden_width, block), F32),
            pltpu.VMEM((hidden_width, wide), BF16),
            pltpu.VMEM((hidden_width, wide), BF16),
        ],
        3 * mat,
    )
    near = jnp.stack([first_near, near_sum(second_term)], 1)
    piece = scatter_sum(near, 0, z_hop, z, z_size)
    pieces = gather_all(piece, y_hop, y, y_size)
    pieces = gather_all(pieces, core_hop, core, cores)
    totals = pieces.transpose(2, 1, 0, 3, 4).reshape(2, rows, hidden_width)

    bias_sum = sum_all(bias_sum, z_hop, z_size)
    bias_len = bias_first.shape[0]
    bias_total = lax.dynamic_slice_in_dim(bias_sum, fsdp_index * bias_len, bias_len, 0)
    return (hidden_new, totals[0], totals[1], bias_total)


def solution(mesh):
    return jax.shard_map(
        on_device,
        mesh=mesh,
        in_specs=(
            P(("dom", "fsdp"), None, None),
            P("dom", "fsdp", None),
            P("dom", "fsdp", None),
            P("dom", None, None),
            P("dom", None),
            P(("dom", "fsdp"), None),
            P(("dom", "fsdp")),
            P(("dom", "fsdp"), None, None, None),
            P("fsdp", None),
            P("fsdp", None),
            P("fsdp"),
            P(("dom", "fsdp"), None, None),
        ),
        out_specs=(P(("dom", "fsdp"), None, None), P("fsdp", None), P("fsdp", None), P("fsdp")),
        check_vma=False,
    )
```

```python
import functools

import jax
import jax.numpy as jnp
from jax import lax
from jax.experimental import pallas as pl
from jax.experimental.pallas import tpu as pltpu
from jax.sharding import PartitionSpec as P

F32 = jnp.float32
BF16 = jnp.bfloat16
CHUNK = 256
VMEM_BYTES = 48 * 1024 * 1024
LAST = (((1,), (1,)), ((), ()))


def add_sources(v, src_ref, cnt_ref, own_ref, arr_ref, tiles_ref, acc):
    own_count = own_ref.shape[0]
    parts = arr_ref.shape[0]
    acc[...] = jnp.zeros_like(acc)

    def step(t, carry):
        source = src_ref[v, t]
        tile = tiles_ref[v, t]

        @pl.when(source < own_count)
        def _():
            acc[...] += jnp.dot(own_ref[source], tile, preferred_element_type=F32)

        @pl.when(source >= own_count)
        def _():
            slot = source - own_count
            block = arr_ref[lax.rem(slot, parts), :, lax.div(slot, parts)]
            block = block.reshape(acc.shape)
            acc[...] += jnp.dot(block, tile, preferred_element_type=F32)

        return carry

    lax.fori_loop(0, cnt_ref[v], step, 0)


def outer_kernel_loop(left, right, out_ref):
    @pl.loop(0, left.shape[0] // CHUNK)
    def _(r):
        rows = pl.ds(pl.multiple_of(r * CHUNK, CHUNK), CHUNK)
        out_ref[rows, :] = lax.dot_general(
            left[rows, :], right[...], LAST, preferred_element_type=F32
        )


def back_kernel(src_ref, cnt_ref, w_ref, grad_ref, tiles_ref, out_ref, wide, second):
    count, _, block = grad_ref.shape
    for v in range(count):
        wide[:, v * block : (v + 1) * block] = grad_ref[v]

    @pl.loop(0, w_ref.shape[0] // CHUNK)
    def _(r):
        rows = pl.ds(pl.multiple_of(r * CHUNK, CHUNK), CHUNK)
        product = jnp.dot(w_ref[rows, :], wide[...], preferred_element_type=F32).astype(BF16)
        for v in range(count):
            second[v, rows, :] = product[:, v * block : (v + 1) * block]

    out_ref[...] = jnp.zeros_like(out_ref)
    for v in range(count):

        def step(t, carry, v=v):
            source = src_ref[v, t]

            @pl.when(source < count)
            def _():
                out_ref[source] += lax.dot_general(
                    second[v], tiles_ref[v, t], LAST, preferred_element_type=F32
                )

            return carry

        lax.fori_loop(0, cnt_ref[v], step, 0)


def first_kernel(
    src_ref, cnt_ref, own_ref, arr_ref, tiles_ref, w_ref, bias_ref, back_ref,
    hidden_ref, grad_ref, sum_ref, acc, agg, pre_grad,
):
    count, _, block = own_ref.shape
    for v in range(count):
        add_sources(v, src_ref, cnt_ref, own_ref, arr_ref, tiles_ref, acc)
        agg[:, v * block : (v + 1) * block] = acc[...].astype(BF16)

    @pl.loop(0, w_ref.shape[0] // CHUNK)
    def _(r):
        rows = pl.ds(pl.multiple_of(r * CHUNK, CHUNK), CHUNK)
        x = jnp.dot(w_ref[rows, :], agg[...], preferred_element_type=F32) + bias_ref[rows, :]
        square = x * x
        bent = jnp.tanh(0.7978845608028654 * x * (1.0 + 0.044715 * square))
        half = 0.5 + 0.5 * bent
        hidden = (x * half).astype(BF16)
        slope = half + 0.5 * x * (1.0 - bent * bent) * (
            0.7978845608028654 * (1.0 + 3.0 * 0.044715 * square)
        )
        for v in range(count):
            columns = slice(v * block, (v + 1) * block)
            hidden_ref[v, rows, :] = hidden[:, columns]
            pre_grad[rows, columns] = (back_ref[v, rows, :] * slope[:, columns]).astype(BF16)

    outer_kernel_loop(agg, pre_grad, grad_ref)
    ones = jnp.ones((sum_ref.shape[0], pre_grad.shape[1]), BF16)
    sum_ref[...] = lax.dot_general(ones, pre_grad[...], LAST, preferred_element_type=F32)


def second_kernel(
    src_ref, cnt_ref, own_ref, arr_ref, tiles_ref, cot_ref, grad_ref, acc, agg, wide
):
    count, _, block = own_ref.shape
    for v in range(count):
        add_sources(v, src_ref, cnt_ref, own_ref, arr_ref, tiles_ref, acc)
        agg[:, v * block : (v + 1) * block] = acc[...].astype(BF16)
        wide[:, v * block : (v + 1) * block] = cot_ref[v]
    outer_kernel_loop(agg, wide, grad_ref)


def local_call(kernel, name, scalars, operands, out_shape, scratch, flops):
    in_specs = [pl.BlockSpec(memory_space=pltpu.SMEM)] * len(scalars)
    in_specs += [pl.BlockSpec(memory_space=pltpu.VMEM)] * len(operands)
    moved = sum(a.size * a.dtype.itemsize for a in operands)
    return pl.pallas_call(
        kernel,
        name=name,
        out_shape=out_shape,
        in_specs=in_specs,
        out_specs=jax.tree.map(lambda _: pl.BlockSpec(memory_space=pltpu.VMEM), out_shape),
        scratch_shapes=scratch,
        compiler_params=pltpu.CompilerParams(vmem_limit_bytes=VMEM_BYTES),
        cost_estimate=pl.CostEstimate(flops=flops, bytes_accessed=moved * 2, transcendentals=0),
    )(*scalars, *operands)


def shifted(axis_name, size, stride, length, k):
    pairs = []
    for index in range(size):
        digit = index // stride % length
        pairs.append((index, index + ((digit + k) % length - digit) * stride))
    return functools.partial(lax.ppermute, axis_name=axis_name, perm=pairs)


def scatter_sum(terms, dim, hop, digit, length):
    mine = lax.dynamic_index_in_dim(terms, digit, dim, keepdims=False)
    for k in range(1, length):
        theirs = lax.dynamic_index_in_dim(terms, (digit + k) % length, dim, keepdims=False)
        mine = mine + hop(k)(theirs.astype(BF16)).astype(F32)
    return mine


def gather_all(piece, hop, digit, length):
    whole = jnp.zeros((length,) + piece.shape, piece.dtype)
    whole = lax.dynamic_update_index_in_dim(whole, piece, digit, 0)
    for k in range(1, length):
        whole = lax.dynamic_update_index_in_dim(
            whole, hop(k)(piece), (digit - k + length) % length, 0
        )
    return whole


def sum_all(vector, hop, length):
    total = vector
    for k in range(1, length):
        total = total + hop(k)(vector)
    return total


def on_device(
    features,
    history_first,
    history_second,
    pull_list,
    pull_count,
    tile_src,
    tile_count,
    tile_values,
    w_first,
    w_second,
    bias_first,
    out_grad,
):
    dom_size = lax.axis_size("dom")
    fsdp_size = lax.axis_size("fsdp")
    dom_index = lax.axis_index("dom")
    fsdp_index = lax.axis_index("fsdp")
    cores = 2 if dom_size % 2 == 0 else 1
    y_size = dom_size // cores
    z_size = 4 if fsdp_size % 4 == 0 else 1
    x_size = fsdp_size // z_size
    core, y = dom_index % cores, dom_index // cores
    x, z = fsdp_index % x_size, fsdp_index // x_size

    def core_hop(k):
        return shifted("dom", dom_size, 1, cores, k)

    def y_hop(k):
        return shifted("dom", dom_size, cores, y_size, k)

    def x_hop(k):
        return shifted("fsdp", fsdp_size, 1, x_size, k)

    def z_hop(k):
        return shifted("fsdp", fsdp_size, x_size, z_size, k)

    count, width, block = features.shape
    hidden_width = w_first.shape[1]

    chosen = pull_list[0]
    requesters, cap = chosen.shape
    live = lax.broadcasted_iota(jnp.int32, chosen.shape, 1) < pull_count[0][:, None]

    def picked(table, chosen):
        taken = jnp.take(table, chosen.reshape(-1), axis=0)
        taken = taken.reshape(chosen.shape + table.shape[1:])
        return jnp.where(live[:, :, None, None], taken, jnp.zeros((), table.dtype))

    def pull(sent):
        got = lax.all_to_all(sent, ("dom", "fsdp"), split_axis=0, concat_axis=0, tiled=True)
        return got.reshape(dom_size, fsdp_size, cap, sent.shape[2], block)

    rows = w_first.shape[0]
    share = rows // dom_size
    bias_row = jnp.pad(bias_first[None, :], ((0, 15), (0, hidden_width - bias_first.shape[0])))
    payload = jnp.concatenate(
        [
            lax.dynamic_slice_in_dim(w_first, dom_index * share, share, 0),
            lax.dynamic_slice_in_dim(w_second, dom_index * share, share, 0),
            bias_row,
        ],
        0,
    )
    along = lax.all_gather(payload, "fsdp", axis=0)
    payload, chosen = lax.optimization_barrier((payload, chosen))
    sent_first = picked(history_first, chosen)
    sent_first, chosen = lax.optimization_barrier((sent_first, chosen))
    arrived_first = pull(sent_first)
    sent_second = picked(history_second, chosen)
    bias_full = along[:, 2 * share, : bias_first.shape[0]].reshape(hidden_width)
    both = lax.all_gather(along[:, : 2 * share], "dom", axis=0)
    both = both.reshape(dom_size, fsdp_size, 2, share, hidden_width)
    both = both.transpose(2, 1, 0, 3, 4).reshape(2, width, hidden_width)
    first_turned = both[0].T
    second_full = both[1]

    scalars = (tile_src, tile_count)
    wide = count * block
    mat = 2 * width * hidden_width * wide
    back_hidden = local_call(
        back_kernel,
        "back_to_hidden",
        scalars,
        (second_full, out_grad, tile_values),
        jax.ShapeDtypeStruct((count, hidden_width, block), F32),
        [
            pltpu.VMEM((hidden_width, wide), BF16),
            pltpu.VMEM((count, hidden_width, block), BF16),
        ],
        2 * mat,
    )
    sent_second, arrived_first, first_turned, back_hidden = lax.optimization_barrier(
        (sent_second, arrived_first, first_turned, back_hidden)
    )
    arrived_second = pull(sent_second)
    hidden_new, first_term, bias_rows = local_call(
        first_kernel,
        "first_layer",
        scalars,
        (
            features,
            arrived_first,
            tile_values,
            first_turned,
            bias_full.astype(F32)[:, None],
            back_hidden,
        ),
        (
            jax.ShapeDtypeStruct((count, hidden_width, block), BF16),
            jax.ShapeDtypeStruct((width, hidden_width), F32),
            jax.ShapeDtypeStruct((8, hidden_width), F32),
        ),
        [
            pltpu.VMEM((width, block), F32),
            pltpu.VMEM((width, wide), BF16),
            pltpu.VMEM((hidden_width, wide), BF16),
        ],
        4 * mat,
    )
    def near_sum(term):
        terms = term.reshape(z_size, x_size, y_size, cores, share, hidden_width)
        terms = scatter_sum(terms, 3, core_hop, core, cores)
        cut = hidden_width // 2
        left = scatter_sum(terms[..., :cut], 1, x_hop, x, x_size)
        right = scatter_sum(terms[..., cut:], 2, y_hop, y, y_size)
        left = scatter_sum(left, 1, y_hop, y, y_size)
        right = scatter_sum(right, 1, x_hop, x, x_size)
        return jnp.concatenate([left, right], -1)

    first_near = near_sum(first_term)
    bias_sum = sum_all(bias_rows[0], core_hop, cores)
    bias_sum = sum_all(bias_sum, x_hop, x_size)
    bias_sum = sum_all(bias_sum, y_hop, y_size)
    bias_sum = sum_all(bias_sum, z_hop, z_size)
    hidden_held, arrived_second, first_near, bias_sum = lax.optimization_barrier(
        (hidden_new, arrived_second, first_near, bias_sum)
    )
    second_term = local_call(
        second_kernel,
        "second_layer",
        scalars,
        (hidden_held, arrived_second, tile_values, out_grad),
        jax.ShapeDtypeStruct((hidden_width, hidden_width), F32),
        [
            pltpu.VMEM((hidden_width, block), F32),
            pltpu.VMEM((hidden_width, wide), BF16),
            pltpu.VMEM((hidden_width, wide), BF16),
        ],
        3 * mat,
    )
    near = jnp.stack([first_near, near_sum(second_term)], 1)
    piece = scatter_sum(near, 0, z_hop, z, z_size).astype(BF16)
    pieces = gather_all(piece, y_hop, y, y_size)
    pieces = gather_all(pieces, core_hop, core, cores)
    totals = pieces.transpose(2, 1, 0, 3, 4).reshape(2, rows, hidden_width).astype(F32)

    bias_len = bias_first.shape[0]
    bias_total = lax.dynamic_slice_in_dim(bias_sum, fsdp_index * bias_len, bias_len, 0)
    return (hidden_new, totals[0], totals[1], bias_total)


def solution(mesh):
    return jax.shard_map(
        on_device,
        mesh=mesh,
        in_specs=(
            P(("dom", "fsdp"), None, None),
            P("dom", "fsdp", None),
            P("dom", "fsdp", None),
            P("dom", None, None),
            P("dom", None),
            P(("dom", "fsdp"), None),
            P(("dom", "fsdp")),
            P(("dom", "fsdp"), None, None, None),
            P("fsdp", None),
            P("fsdp", None),
            P("fsdp"),
            P(("dom", "fsdp"), None, None),
        ),
        out_specs=(P(("dom", "fsdp"), None, None), P("fsdp", None), P("fsdp", None), P("fsdp")),
        check_vma=False,
    )
```

```python
import functools

import jax
import jax.numpy as jnp
from jax import lax
from jax.experimental import pallas as pl
from jax.experimental.pallas import tpu as pltpu
from jax.sharding import PartitionSpec as P

F32 = jnp.float32
BF16 = jnp.bfloat16
CHUNK = 256
VMEM_BYTES = 48 * 1024 * 1024
LAST = (((1,), (1,)), ((), ()))


def add_sources(v, src_ref, cnt_ref, own_ref, arr_ref, tiles_ref, acc):
    own_count = own_ref.shape[0]
    parts = arr_ref.shape[0]
    acc[...] = jnp.zeros_like(acc)

    def step(t, carry):
        source = src_ref[v, t]
        tile = tiles_ref[v, t]

        @pl.when(source < own_count)
        def _():
            acc[...] += jnp.dot(own_ref[source], tile, preferred_element_type=F32)

        @pl.when(source >= own_count)
        def _():
            slot = source - own_count
            block = arr_ref[lax.rem(slot, parts), :, lax.div(slot, parts)]
            block = block.reshape(acc.shape)
            acc[...] += jnp.dot(block, tile, preferred_element_type=F32)

        return carry

    lax.fori_loop(0, cnt_ref[v], step, 0)


def outer_kernel_loop(left, right, out_ref):
    @pl.loop(0, left.shape[0] // CHUNK)
    def _(r):
        rows = pl.ds(pl.multiple_of(r * CHUNK, CHUNK), CHUNK)
        out_ref[rows, :] = lax.dot_general(
            left[rows, :], right[...], LAST, preferred_element_type=F32
        )


def back_kernel(src_ref, cnt_ref, w_ref, grad_ref, tiles_ref, out_ref, wide, second):
    count, _, block = grad_ref.shape
    for v in range(count):
        wide[:, v * block : (v + 1) * block] = grad_ref[v]

    @pl.loop(0, w_ref.shape[0] // CHUNK)
    def _(r):
        rows = pl.ds(pl.multiple_of(r * CHUNK, CHUNK), CHUNK)
        product = jnp.dot(w_ref[rows, :], wide[...], preferred_element_type=F32).astype(BF16)
        for v in range(count):
            second[v, rows, :] = product[:, v * block : (v + 1) * block]

    out_ref[...] = jnp.zeros_like(out_ref)
    for v in range(count):

        def step(t, carry, v=v):
            source = src_ref[v, t]

            @pl.when(source < count)
            def _():
                out_ref[source] += lax.dot_general(
                    second[v], tiles_ref[v, t], LAST, preferred_element_type=F32
                )

            return carry

        lax.fori_loop(0, cnt_ref[v], step, 0)


def first_kernel(
    src_ref, cnt_ref, own_ref, arr_ref, tiles_ref, w_ref, bias_ref, back_ref,
    hidden_ref, grad_ref, sum_ref, acc, agg, pre_grad,
):
    count, _, block = own_ref.shape
    for v in range(count):
        add_sources(v, src_ref, cnt_ref, own_ref, arr_ref, tiles_ref, acc)
        agg[:, v * block : (v + 1) * block] = acc[...].astype(BF16)

    @pl.loop(0, w_ref.shape[0] // CHUNK)
    def _(r):
        rows = pl.ds(pl.multiple_of(r * CHUNK, CHUNK), CHUNK)
        x = jnp.dot(w_ref[rows, :], agg[...], preferred_element_type=F32) + bias_ref[rows, :]
        square = x * x
        bent = jnp.tanh(0.7978845608028654 * x * (1.0 + 0.044715 * square))
        half = 0.5 + 0.5 * bent
        hidden = (x * half).astype(BF16)
        slope = half + 0.5 * x * (1.0 - bent * bent) * (
            0.7978845608028654 * (1.0 + 3.0 * 0.044715 * square)
        )
        for v in range(count):
            columns = slice(v * block, (v + 1) * block)
            hidden_ref[v, rows, :] = hidden[:, columns]
            pre_grad[rows, columns] = (back_ref[v, rows, :] * slope[:, columns]).astype(BF16)

    outer_kernel_loop(agg, pre_grad, grad_ref)
    ones = jnp.ones((sum_ref.shape[0], pre_grad.shape[1]), BF16)
    sum_ref[...] = lax.dot_general(ones, pre_grad[...], LAST, preferred_element_type=F32)


def second_kernel(
    src_ref, cnt_ref, own_ref, arr_ref, tiles_ref, cot_ref, grad_ref, acc, agg, wide
):
    count, _, block = own_ref.shape
    for v in range(count):
        add_sources(v, src_ref, cnt_ref, own_ref, arr_ref, tiles_ref, acc)
        agg[:, v * block : (v + 1) * block] = acc[...].astype(BF16)
        wide[:, v * block : (v + 1) * block] = cot_ref[v]
    outer_kernel_loop(agg, wide, grad_ref)


def local_call(kernel, name, scalars, operands, out_shape, scratch, flops):
    in_specs = [pl.BlockSpec(memory_space=pltpu.SMEM)] * len(scalars)
    in_specs += [pl.BlockSpec(memory_space=pltpu.VMEM)] * len(operands)
    moved = sum(a.size * a.dtype.itemsize for a in operands)
    return pl.pallas_call(
        kernel,
        name=name,
        out_shape=out_shape,
        in_specs=in_specs,
        out_specs=jax.tree.map(lambda _: pl.BlockSpec(memory_space=pltpu.VMEM), out_shape),
        scratch_shapes=scratch,
        compiler_params=pltpu.CompilerParams(vmem_limit_bytes=VMEM_BYTES),
        cost_estimate=pl.CostEstimate(flops=flops, bytes_accessed=moved * 2, transcendentals=0),
    )(*scalars, *operands)


def shifted(axis_name, size, stride, length, k):
    pairs = []
    for index in range(size):
        digit = index // stride % length
        pairs.append((index, index + ((digit + k) % length - digit) * stride))
    return functools.partial(lax.ppermute, axis_name=axis_name, perm=pairs)


def scatter_sum(terms, dim, hop, digit, length):
    mine = lax.dynamic_index_in_dim(terms, digit, dim, keepdims=False)
    for k in range(1, length):
        theirs = lax.dynamic_index_in_dim(terms, (digit + k) % length, dim, keepdims=False)
        mine = mine + hop(k)(theirs.astype(BF16)).astype(F32)
    return mine


def gather_all(piece, hop, digit, length):
    whole = jnp.zeros((length,) + piece.shape, piece.dtype)
    whole = lax.dynamic_update_index_in_dim(whole, piece, digit, 0)
    for k in range(1, length):
        whole = lax.dynamic_update_index_in_dim(
            whole, hop(k)(piece), (digit - k + length) % length, 0
        )
    return whole


def sum_all(vector, hop, length):
    total = vector
    for k in range(1, length):
        total = total + hop(k)(vector)
    return total


def on_device(
    features,
    history_first,
    history_second,
    pull_list,
    pull_count,
    tile_src,
    tile_count,
    tile_values,
    w_first,
    w_second,
    bias_first,
    out_grad,
):
    dom_size = lax.axis_size("dom")
    fsdp_size = lax.axis_size("fsdp")
    dom_index = lax.axis_index("dom")
    fsdp_index = lax.axis_index("fsdp")
    cores = 2 if dom_size % 2 == 0 else 1
    y_size = dom_size // cores
    z_size = 4 if fsdp_size % 4 == 0 else 1
    x_size = fsdp_size // z_size
    core, y = dom_index % cores, dom_index // cores
    x, z = fsdp_index % x_size, fsdp_index // x_size

    def core_hop(k):
        return shifted("dom", dom_size, 1, cores, k)

    def y_hop(k):
        return shifted("dom", dom_size, cores, y_size, k)

    def x_hop(k):
        return shifted("fsdp", fsdp_size, 1, x_size, k)

    def z_hop(k):
        return shifted("fsdp", fsdp_size, x_size, z_size, k)

    count, width, block = features.shape
    hidden_width = w_first.shape[1]

    chosen = pull_list[0]
    requesters, cap = chosen.shape
    live = lax.broadcasted_iota(jnp.int32, chosen.shape, 1) < pull_count[0][:, None]

    def picked(table, chosen):
        taken = jnp.take(table, chosen.reshape(-1), axis=0)
        taken = taken.reshape(chosen.shape + table.shape[1:])
        return jnp.where(live[:, :, None, None], taken, jnp.zeros((), table.dtype))

    def pull(sent):
        got = lax.all_to_all(sent, ("dom", "fsdp"), split_axis=0, concat_axis=0, tiled=True)
        return got.reshape(dom_size, fsdp_size, cap, sent.shape[2], block)

    rows = w_first.shape[0]
    share = rows // dom_size
    bias_row = jnp.pad(bias_first[None, :], ((0, 15), (0, hidden_width - bias_first.shape[0])))
    payload = jnp.concatenate(
        [
            lax.dynamic_slice_in_dim(w_first, dom_index * share, share, 0),
            lax.dynamic_slice_in_dim(w_second, dom_index * share, share, 0),
            bias_row,
        ],
        0,
    )
    along = lax.all_gather(payload, "fsdp", axis=0)
    payload, chosen = lax.optimization_barrier((payload, chosen))
    sent_first = picked(history_first, chosen)
    sent_first, chosen = lax.optimization_barrier((sent_first, chosen))
    arrived_first = pull(sent_first)
    sent_second = picked(history_second, chosen)
    bias_full = along[:, 2 * share, : bias_first.shape[0]].reshape(hidden_width)
    both = lax.all_gather(along[:, : 2 * share], "dom", axis=0)
    both = both.reshape(dom_size, fsdp_size, 2, share, hidden_width)
    both = both.transpose(2, 1, 0, 3, 4).reshape(2, width, hidden_width)
    first_turned = both[0].T
    second_full = both[1]

    scalars = (tile_src, tile_count)
    wide = count * block
    mat = 2 * width * hidden_width * wide
    back_hidden = local_call(
        back_kernel,
        "back_to_hidden",
        scalars,
        (second_full, out_grad, tile_values),
        jax.ShapeDtypeStruct((count, hidden_width, block), F32),
        [
            pltpu.VMEM((hidden_width, wide), BF16),
            pltpu.VMEM((count, hidden_width, block), BF16),
        ],
        2 * mat,
    )
    sent_second, arrived_first = lax.optimization_barrier((sent_second, arrived_first))
    arrived_second = pull(sent_second)
    hidden_new, first_term, bias_rows = local_call(
        first_kernel,
        "first_layer",
        scalars,
        (
            features,
            arrived_first,
            tile_values,
            first_turned,
            bias_full.astype(F32)[:, None],
            back_hidden,
        ),
        (
            jax.ShapeDtypeStruct((count, hidden_width, block), BF16),
            jax.ShapeDtypeStruct((width, hidden_width), F32),
            jax.ShapeDtypeStruct((8, hidden_width), F32),
        ),
        [
            pltpu.VMEM((width, block), F32),
            pltpu.VMEM((width, wide), BF16),
            pltpu.VMEM((hidden_width, wide), BF16),
        ],
        4 * mat,
    )
    def near_sum(term, split):
        terms = term.reshape(z_size, x_size, y_size, cores, share, hidden_width)
        terms = scatter_sum(terms, 3, core_hop, core, cores)
        if not split:
            terms = scatter_sum(terms, 1, x_hop, x, x_size)
            return scatter_sum(terms, 1, y_hop, y, y_size)
        cut = hidden_width // 2
        left = scatter_sum(terms[..., :cut], 1, x_hop, x, x_size)
        right = scatter_sum(terms[..., cut:], 2, y_hop, y, y_size)
        left = scatter_sum(left, 1, y_hop, y, y_size)
        right = scatter_sum(right, 1, x_hop, x, x_size)
        return jnp.concatenate([left, right], -1)

    first_near = near_sum(first_term, False)
    bias_sum = sum_all(bias_rows[0], core_hop, cores)
    bias_sum = sum_all(bias_sum, x_hop, x_size)
    bias_sum = sum_all(bias_sum, y_hop, y_size)
    hidden_held, arrived_second, first_near, bias_sum = lax.optimization_barrier(
        (hidden_new, arrived_second, first_near, bias_sum)
    )
    second_term = local_call(
        second_kernel,
        "second_layer",
        scalars,
        (hidden_held, arrived_second, tile_values, out_grad),
        jax.ShapeDtypeStruct((hidden_width, hidden_width), F32),
        [
            pltpu.VMEM((hidden_width, block), F32),
            pltpu.VMEM((hidden_width, wide), BF16),
            pltpu.VMEM((hidden_width, wide), BF16),
        ],
        3 * mat,
    )
    bias_rows = jnp.pad(bias_sum.reshape(z_size, 1, -1), ((0, 0), (0, 7), (0, 0)))
    bias_rows = jnp.pad(
        bias_rows, ((0, 0), (0, 0), (0, hidden_width - hidden_width // z_size))
    )
    near = jnp.concatenate([first_near, near_sum(second_term, True), bias_rows], 1)
    piece = scatter_sum(near, 0, z_hop, z, z_size)
    bias_len = bias_first.shape[0]
    bias_total = lax.dynamic_slice_in_dim(piece[2 * share], x * bias_len, bias_len, 0)
    piece = piece[: 2 * share].astype(BF16).reshape(2, share, hidden_width)
    pieces = gather_all(piece, y_hop, y, y_size)
    pieces = gather_all(pieces, core_hop, core, cores)
    totals = pieces.transpose(2, 1, 0, 3, 4).reshape(2, rows, hidden_width).astype(F32)
    return (hidden_new, totals[0], totals[1], bias_total)


def solution(mesh):
    return jax.shard_map(
        on_device,
        mesh=mesh,
        in_specs=(
            P(("dom", "fsdp"), None, None),
            P("dom", "fsdp", None),
            P("dom", "fsdp", None),
            P("dom", None, None),
            P("dom", None),
            P(("dom", "fsdp"), None),
            P(("dom", "fsdp")),
            P(("dom", "fsdp"), None, None, None),
            P("fsdp", None),
            P("fsdp", None),
            P("fsdp"),
            P(("dom", "fsdp"), None, None),
        ),
        out_specs=(P(("dom", "fsdp"), None, None), P("fsdp", None), P("fsdp", None), P("fsdp")),
        check_vma=False,
    )
```

```python
import functools

import jax
import jax.numpy as jnp
from jax import lax
from jax.experimental import pallas as pl
from jax.experimental.pallas import tpu as pltpu
from jax.sharding import PartitionSpec as P

F32 = jnp.float32
BF16 = jnp.bfloat16
CHUNK = 256
VMEM_BYTES = 48 * 1024 * 1024
LAST = (((1,), (1,)), ((), ()))


def add_sources(v, src_ref, cnt_ref, own_ref, arr_ref, tiles_ref, acc):
    own_count = own_ref.shape[0]
    parts = arr_ref.shape[0]
    acc[...] = jnp.zeros_like(acc)

    def step(t, carry):
        source = src_ref[v, t]
        tile = tiles_ref[v, t]

        @pl.when(source < own_count)
        def _():
            acc[...] += jnp.dot(own_ref[source], tile, preferred_element_type=F32)

        @pl.when(source >= own_count)
        def _():
            slot = source - own_count
            block = arr_ref[lax.rem(slot, parts), :, lax.div(slot, parts)]
            block = block.reshape(acc.shape)
            acc[...] += jnp.dot(block, tile, preferred_element_type=F32)

        return carry

    lax.fori_loop(0, cnt_ref[v], step, 0)


def outer_kernel_loop(left, right, out_ref):
    @pl.loop(0, left.shape[0] // CHUNK)
    def _(r):
        rows = pl.ds(pl.multiple_of(r * CHUNK, CHUNK), CHUNK)
        out_ref[rows, :] = lax.dot_general(
            left[rows, :], right[...], LAST, preferred_element_type=F32
        )


def back_kernel(src_ref, cnt_ref, w_ref, grad_ref, tiles_ref, out_ref, wide, second):
    count, _, block = grad_ref.shape
    for v in range(count):
        wide[:, v * block : (v + 1) * block] = grad_ref[v]

    @pl.loop(0, w_ref.shape[0] // CHUNK)
    def _(r):
        rows = pl.ds(pl.multiple_of(r * CHUNK, CHUNK), CHUNK)
        product = jnp.dot(w_ref[rows, :], wide[...], preferred_element_type=F32).astype(BF16)
        for v in range(count):
            second[v, rows, :] = product[:, v * block : (v + 1) * block]

    out_ref[...] = jnp.zeros_like(out_ref)
    for v in range(count):

        def step(t, carry, v=v):
            source = src_ref[v, t]

            @pl.when(source < count)
            def _():
                out_ref[source] += lax.dot_general(
                    second[v], tiles_ref[v, t], LAST, preferred_element_type=F32
                )

            return carry

        lax.fori_loop(0, cnt_ref[v], step, 0)


def first_kernel(
    src_ref, cnt_ref, own_ref, arr_ref, tiles_ref, w_ref, bias_ref, back_ref,
    hidden_ref, grad_ref, sum_ref, acc, agg, pre_grad,
):
    count, _, block = own_ref.shape
    for v in range(count):
        add_sources(v, src_ref, cnt_ref, own_ref, arr_ref, tiles_ref, acc)
        agg[:, v * block : (v + 1) * block] = acc[...].astype(BF16)

    @pl.loop(0, w_ref.shape[0] // CHUNK)
    def _(r):
        rows = pl.ds(pl.multiple_of(r * CHUNK, CHUNK), CHUNK)
        x = jnp.dot(w_ref[rows, :], agg[...], preferred_element_type=F32) + bias_ref[rows, :]
        square = x * x
        bent = jnp.tanh(0.7978845608028654 * x * (1.0 + 0.044715 * square))
        half = 0.5 + 0.5 * bent
        hidden = (x * half).astype(BF16)
        slope = half + 0.5 * x * (1.0 - bent * bent) * (
            0.7978845608028654 * (1.0 + 3.0 * 0.044715 * square)
        )
        for v in range(count):
            columns = slice(v * block, (v + 1) * block)
            hidden_ref[v, rows, :] = hidden[:, columns]
            pre_grad[rows, columns] = (back_ref[v, rows, :] * slope[:, columns]).astype(BF16)

    outer_kernel_loop(agg, pre_grad, grad_ref)
    ones = jnp.ones((sum_ref.shape[0], pre_grad.shape[1]), BF16)
    sum_ref[...] = lax.dot_general(ones, pre_grad[...], LAST, preferred_element_type=F32)


def second_kernel(
    src_ref, cnt_ref, own_ref, arr_ref, tiles_ref, cot_ref, grad_ref, acc, agg, wide
):
    count, _, block = own_ref.shape
    for v in range(count):
        add_sources(v, src_ref, cnt_ref, own_ref, arr_ref, tiles_ref, acc)
        agg[:, v * block : (v + 1) * block] = acc[...].astype(BF16)
        wide[:, v * block : (v + 1) * block] = cot_ref[v]
    outer_kernel_loop(agg, wide, grad_ref)


def local_call(kernel, name, scalars, operands, out_shape, scratch, flops):
    in_specs = [pl.BlockSpec(memory_space=pltpu.SMEM)] * len(scalars)
    in_specs += [pl.BlockSpec(memory_space=pltpu.VMEM)] * len(operands)
    moved = sum(a.size * a.dtype.itemsize for a in operands)
    return pl.pallas_call(
        kernel,
        name=name,
        out_shape=out_shape,
        in_specs=in_specs,
        out_specs=jax.tree.map(lambda _: pl.BlockSpec(memory_space=pltpu.VMEM), out_shape),
        scratch_shapes=scratch,
        compiler_params=pltpu.CompilerParams(vmem_limit_bytes=VMEM_BYTES),
        cost_estimate=pl.CostEstimate(flops=flops, bytes_accessed=moved * 2, transcendentals=0),
    )(*scalars, *operands)


def shifted(axis_name, size, stride, length, k):
    pairs = []
    for index in range(size):
        digit = index // stride % length
        pairs.append((index, index + ((digit + k) % length - digit) * stride))
    return functools.partial(lax.ppermute, axis_name=axis_name, perm=pairs)


def scatter_sum(terms, dim, hop, digit, length):
    mine = lax.dynamic_index_in_dim(terms, digit, dim, keepdims=False)
    for k in range(1, length):
        theirs = lax.dynamic_index_in_dim(terms, (digit + k) % length, dim, keepdims=False)
        mine = mine + hop(k)(theirs.astype(BF16)).astype(F32)
    return mine


def gather_all(piece, hop, digit, length):
    whole = jnp.zeros((length,) + piece.shape, piece.dtype)
    whole = lax.dynamic_update_index_in_dim(whole, piece, digit, 0)
    for k in range(1, length):
        whole = lax.dynamic_update_index_in_dim(
            whole, hop(k)(piece), (digit - k + length) % length, 0
        )
    return whole


def sum_all(vector, hop, length):
    total = vector
    for k in range(1, length):
        total = total + hop(k)(vector)
    return total


def on_device(
    features,
    history_first,
    history_second,
    pull_list,
    pull_count,
    tile_src,
    tile_count,
    tile_values,
    w_first,
    w_second,
    bias_first,
    out_grad,
):
    dom_size = lax.axis_size("dom")
    fsdp_size = lax.axis_size("fsdp")
    dom_index = lax.axis_index("dom")
    fsdp_index = lax.axis_index("fsdp")
    cores = 2 if dom_size % 2 == 0 else 1
    y_size = dom_size // cores
    z_size = 4 if fsdp_size % 4 == 0 else 1
    x_size = fsdp_size // z_size
    core, y = dom_index % cores, dom_index // cores
    x, z = fsdp_index % x_size, fsdp_index // x_size

    def core_hop(k):
        return shifted("dom", dom_size, 1, cores, k)

    def y_hop(k):
        return shifted("dom", dom_size, cores, y_size, k)

    def x_hop(k):
        return shifted("fsdp", fsdp_size, 1, x_size, k)

    def z_hop(k):
        return shifted("fsdp", fsdp_size, x_size, z_size, k)

    count, width, block = features.shape
    hidden_width = w_first.shape[1]

    chosen = pull_list[0]
    requesters, cap = chosen.shape
    live = lax.broadcasted_iota(jnp.int32, chosen.shape, 1) < pull_count[0][:, None]

    def picked(table, chosen):
        taken = jnp.take(table, chosen.reshape(-1), axis=0)
        taken = taken.reshape(chosen.shape + table.shape[1:])
        return jnp.where(live[:, :, None, None], taken, jnp.zeros((), table.dtype))

    def pull(sent):
        got = lax.all_to_all(sent, ("dom", "fsdp"), split_axis=0, concat_axis=0, tiled=True)
        return got.reshape(dom_size, fsdp_size, cap, sent.shape[2], block)

    rows = w_first.shape[0]
    share = rows // dom_size
    bias_row = jnp.pad(bias_first[None, :], ((0, 15), (0, hidden_width - bias_first.shape[0])))
    payload = jnp.concatenate(
        [
            lax.dynamic_slice_in_dim(w_first, dom_index * share, share, 0),
            lax.dynamic_slice_in_dim(w_second, dom_index * share, share, 0),
            bias_row,
        ],
        0,
    )
    along = lax.all_gather(payload, "fsdp", axis=0)
    payload, chosen = lax.optimization_barrier((payload, chosen))
    sent_first = picked(history_first, chosen)
    sent_first, chosen = lax.optimization_barrier((sent_first, chosen))
    arrived_first = pull(sent_first)
    sent_second = picked(history_second, chosen)
    bias_full = along[:, 2 * share, : bias_first.shape[0]].reshape(hidden_width)
    both = lax.all_gather(along[:, : 2 * share], "dom", axis=0)
    both = both.reshape(dom_size, fsdp_size, 2, share, hidden_width)
    both = both.transpose(2, 1, 0, 3, 4).reshape(2, width, hidden_width)
    first_turned = both[0].T
    second_full = both[1]

    scalars = (tile_src, tile_count)
    wide = count * block
    mat = 2 * width * hidden_width * wide
    back_hidden = local_call(
        back_kernel,
        "back_to_hidden",
        scalars,
        (second_full, out_grad, tile_values),
        jax.ShapeDtypeStruct((count, hidden_width, block), F32),
        [
            pltpu.VMEM((hidden_width, wide), BF16),
            pltpu.VMEM((count, hidden_width, block), BF16),
        ],
        2 * mat,
    )
    sent_second, arrived_first = lax.optimization_barrier((sent_second, arrived_first))
    arrived_second = pull(sent_second)
    hidden_new, first_term, bias_rows = local_call(
        first_kernel,
        "first_layer",
        scalars,
        (
            features,
            arrived_first,
            tile_values,
            first_turned,
            bias_full.astype(F32)[:, None],
            back_hidden,
        ),
        (
            jax.ShapeDtypeStruct((count, hidden_width, block), BF16),
            jax.ShapeDtypeStruct((width, hidden_width), F32),
            jax.ShapeDtypeStruct((8, hidden_width), F32),
        ),
        [
            pltpu.VMEM((width, block), F32),
            pltpu.VMEM((width, wide), BF16),
            pltpu.VMEM((hidden_width, wide), BF16),
        ],
        4 * mat,
    )
    def near_sum(term, split):
        terms = term.reshape(z_size, x_size, y_size, cores, share, hidden_width)
        terms = scatter_sum(terms, 3, core_hop, core, cores)
        if not split:
            terms = scatter_sum(terms, 1, x_hop, x, x_size)
            return scatter_sum(terms, 1, y_hop, y, y_size)
        cut = hidden_width // 2
        left = scatter_sum(terms[..., :cut], 1, x_hop, x, x_size)
        right = scatter_sum(terms[..., cut:], 2, y_hop, y, y_size)
        left = scatter_sum(left, 1, y_hop, y, y_size)
        right = scatter_sum(right, 1, x_hop, x, x_size)
        return jnp.concatenate([left, right], -1)

    first_near = near_sum(first_term, False)
    bias_sum = sum_all(bias_rows[0], core_hop, cores)
    bias_sum = sum_all(bias_sum, x_hop, x_size)
    bias_sum = sum_all(bias_sum, y_hop, y_size)
    hidden_held, arrived_second, first_near = lax.optimization_barrier(
        (hidden_new, arrived_second, first_near)
    )
    second_term = local_call(
        second_kernel,
        "second_layer",
        scalars,
        (hidden_held, arrived_second, tile_values, out_grad),
        jax.ShapeDtypeStruct((hidden_width, hidden_width), F32),
        [
            pltpu.VMEM((hidden_width, block), F32),
            pltpu.VMEM((hidden_width, wide), BF16),
            pltpu.VMEM((hidden_width, wide), BF16),
        ],
        3 * mat,
    )
    bias_rows = jnp.pad(bias_sum.reshape(z_size, 1, -1), ((0, 0), (0, 7), (0, 0)))
    bias_rows = jnp.pad(
        bias_rows, ((0, 0), (0, 0), (0, hidden_width - hidden_width // z_size))
    )
    near = jnp.concatenate([first_near, near_sum(second_term, True), bias_rows], 1)
    piece = scatter_sum(near, 0, z_hop, z, z_size)
    bias_len = bias_first.shape[0]
    bias_total = lax.dynamic_slice_in_dim(piece[2 * share], x * bias_len, bias_len, 0)
    piece = piece[: 2 * share].astype(BF16).reshape(2, share, hidden_width)
    pieces = gather_all(piece, y_hop, y, y_size)
    pieces = gather_all(pieces, core_hop, core, cores)
    totals = pieces.transpose(2, 1, 0, 3, 4).reshape(2, rows, hidden_width).astype(F32)
    return (hidden_new, totals[0], totals[1], bias_total)


def solution(mesh):
    return jax.shard_map(
        on_device,
        mesh=mesh,
        in_specs=(
            P(("dom", "fsdp"), None, None),
            P("dom", "fsdp", None),
            P("dom", "fsdp", None),
            P("dom", None, None),
            P("dom", None),
            P(("dom", "fsdp"), None),
            P(("dom", "fsdp")),
            P(("dom", "fsdp"), None, None, None),
            P("fsdp", None),
            P("fsdp", None),
            P("fsdp"),
            P(("dom", "fsdp"), None, None),
        ),
        out_specs=(P(("dom", "fsdp"), None, None), P("fsdp", None), P("fsdp", None), P("fsdp")),
        check_vma=False,
    )
```

```python
import functools

import jax
import jax.numpy as jnp
from jax import lax
from jax.experimental import pallas as pl
from jax.experimental.pallas import tpu as pltpu
from jax.sharding import PartitionSpec as P

F32 = jnp.float32
BF16 = jnp.bfloat16
CHUNK = 256
VMEM_BYTES = 48 * 1024 * 1024
LAST = (((1,), (1,)), ((), ()))


def add_sources(v, src_ref, cnt_ref, own_ref, arr_ref, tiles_ref, acc):
    own_count = own_ref.shape[0]
    parts = arr_ref.shape[0]
    acc[...] = jnp.zeros_like(acc)

    def step(t, carry):
        source = src_ref[v, t]
        tile = tiles_ref[v, t]

        @pl.when(source < own_count)
        def _():
            acc[...] += jnp.dot(own_ref[source], tile, preferred_element_type=F32)

        @pl.when(source >= own_count)
        def _():
            slot = source - own_count
            block = arr_ref[lax.rem(slot, parts), :, lax.div(slot, parts)]
            block = block.reshape(acc.shape)
            acc[...] += jnp.dot(block, tile, preferred_element_type=F32)

        return carry

    lax.fori_loop(0, cnt_ref[v], step, 0)


def outer_kernel_loop(left, right, out_ref):
    @pl.loop(0, left.shape[0] // CHUNK)
    def _(r):
        rows = pl.ds(pl.multiple_of(r * CHUNK, CHUNK), CHUNK)
        out_ref[rows, :] = lax.dot_general(
            left[rows, :], right[...], LAST, preferred_element_type=F32
        )


def back_kernel(src_ref, cnt_ref, w_ref, grad_ref, tiles_ref, out_ref, wide, second):
    count, _, block = grad_ref.shape
    for v in range(count):
        wide[:, v * block : (v + 1) * block] = grad_ref[v]

    @pl.loop(0, w_ref.shape[0] // CHUNK)
    def _(r):
        rows = pl.ds(pl.multiple_of(r * CHUNK, CHUNK), CHUNK)
        product = jnp.dot(w_ref[rows, :], wide[...], preferred_element_type=F32).astype(BF16)
        for v in range(count):
            second[v, rows, :] = product[:, v * block : (v + 1) * block]

    out_ref[...] = jnp.zeros_like(out_ref)
    for v in range(count):

        def step(t, carry, v=v):
            source = src_ref[v, t]

            @pl.when(source < count)
            def _():
                out_ref[source] += lax.dot_general(
                    second[v], tiles_ref[v, t], LAST, preferred_element_type=F32
                )

            return carry

        lax.fori_loop(0, cnt_ref[v], step, 0)


def first_kernel(
    src_ref, cnt_ref, own_ref, arr_ref, tiles_ref, w_ref, bias_ref, back_ref,
    hidden_ref, grad_ref, sum_ref, acc, agg, pre_grad,
):
    count, _, block = own_ref.shape
    for v in range(count):
        add_sources(v, src_ref, cnt_ref, own_ref, arr_ref, tiles_ref, acc)
        agg[:, v * block : (v + 1) * block] = acc[...].astype(BF16)

    @pl.loop(0, w_ref.shape[0] // CHUNK)
    def _(r):
        rows = pl.ds(pl.multiple_of(r * CHUNK, CHUNK), CHUNK)
        x = jnp.dot(w_ref[rows, :], agg[...], preferred_element_type=F32) + bias_ref[rows, :]
        square = x * x
        bent = jnp.tanh(0.7978845608028654 * x * (1.0 + 0.044715 * square))
        half = 0.5 + 0.5 * bent
        hidden = (x * half).astype(BF16)
        slope = half + 0.5 * x * (1.0 - bent * bent) * (
            0.7978845608028654 * (1.0 + 3.0 * 0.044715 * square)
        )
        for v in range(count):
            columns = slice(v * block, (v + 1) * block)
            hidden_ref[v, rows, :] = hidden[:, columns]
            pre_grad[rows, columns] = (back_ref[v, rows, :] * slope[:, columns]).astype(BF16)

    outer_kernel_loop(agg, pre_grad, grad_ref)
    ones = jnp.ones((sum_ref.shape[0], pre_grad.shape[1]), BF16)
    sum_ref[...] = lax.dot_general(ones, pre_grad[...], LAST, preferred_element_type=F32)


def second_kernel(
    src_ref, cnt_ref, own_ref, arr_ref, tiles_ref, cot_ref, grad_ref, acc, agg, wide
):
    count, _, block = own_ref.shape
    for v in range(count):
        add_sources(v, src_ref, cnt_ref, own_ref, arr_ref, tiles_ref, acc)
        agg[:, v * block : (v + 1) * block] = acc[...].astype(BF16)
        wide[:, v * block : (v + 1) * block] = cot_ref[v]
    outer_kernel_loop(agg, wide, grad_ref)


def local_call(kernel, name, scalars, operands, out_shape, scratch, flops):
    in_specs = [pl.BlockSpec(memory_space=pltpu.SMEM)] * len(scalars)
    in_specs += [pl.BlockSpec(memory_space=pltpu.VMEM)] * len(operands)
    moved = sum(a.size * a.dtype.itemsize for a in operands)
    return pl.pallas_call(
        kernel,
        name=name,
        out_shape=out_shape,
        in_specs=in_specs,
        out_specs=jax.tree.map(lambda _: pl.BlockSpec(memory_space=pltpu.VMEM), out_shape),
        scratch_shapes=scratch,
        compiler_params=pltpu.CompilerParams(vmem_limit_bytes=VMEM_BYTES),
        cost_estimate=pl.CostEstimate(flops=flops, bytes_accessed=moved * 2, transcendentals=0),
    )(*scalars, *operands)


def shifted(axis_name, size, stride, length, k):
    pairs = []
    for index in range(size):
        digit = index // stride % length
        pairs.append((index, index + ((digit + k) % length - digit) * stride))
    return functools.partial(lax.ppermute, axis_name=axis_name, perm=pairs)


def scatter_sum(terms, dim, hop, digit, length):
    mine = lax.dynamic_index_in_dim(terms, digit, dim, keepdims=False)
    for k in range(1, length):
        theirs = lax.dynamic_index_in_dim(terms, (digit + k) % length, dim, keepdims=False)
        mine = mine + hop(k)(theirs.astype(BF16)).astype(F32)
    return mine


def gather_all(piece, hop, digit, length):
    whole = jnp.zeros((length,) + piece.shape, piece.dtype)
    whole = lax.dynamic_update_index_in_dim(whole, piece, digit, 0)
    for k in range(1, length):
        whole = lax.dynamic_update_index_in_dim(
            whole, hop(k)(piece), (digit - k + length) % length, 0
        )
    return whole


def sum_all(vector, hop, length):
    total = vector
    for k in range(1, length):
        total = total + hop(k)(vector)
    return total


def on_device(
    features,
    history_first,
    history_second,
    pull_list,
    pull_count,
    tile_src,
    tile_count,
    tile_values,
    w_first,
    w_second,
    bias_first,
    out_grad,
):
    dom_size = lax.axis_size("dom")
    fsdp_size = lax.axis_size("fsdp")
    dom_index = lax.axis_index("dom")
    fsdp_index = lax.axis_index("fsdp")
    cores = 2 if dom_size % 2 == 0 else 1
    y_size = dom_size // cores
    z_size = 4 if fsdp_size % 4 == 0 else 1
    x_size = fsdp_size // z_size
    core, y = dom_index % cores, dom_index // cores
    x, z = fsdp_index % x_size, fsdp_index // x_size

    def core_hop(k):
        return shifted("dom", dom_size, 1, cores, k)

    def y_hop(k):
        return shifted("dom", dom_size, cores, y_size, k)

    def x_hop(k):
        return shifted("fsdp", fsdp_size, 1, x_size, k)

    def z_hop(k):
        return shifted("fsdp", fsdp_size, x_size, z_size, k)

    count, width, block = features.shape
    hidden_width = w_first.shape[1]

    chosen = pull_list[0]
    requesters, cap = chosen.shape
    live = lax.broadcasted_iota(jnp.int32, chosen.shape, 1) < pull_count[0][:, None]

    def picked(table, chosen):
        taken = jnp.take(table, chosen.reshape(-1), axis=0)
        taken = taken.reshape(chosen.shape + table.shape[1:])
        return jnp.where(live[:, :, None, None], taken, jnp.zeros((), table.dtype))

    def pull(sent):
        got = lax.all_to_all(sent, ("dom", "fsdp"), split_axis=0, concat_axis=0, tiled=True)
        return got.reshape(dom_size, fsdp_size, cap, sent.shape[2], block)

    rows = w_first.shape[0]
    share = rows // dom_size
    bias_row = jnp.pad(bias_first[None, :], ((0, 15), (0, hidden_width - bias_first.shape[0])))
    payload = jnp.concatenate(
        [
            lax.dynamic_slice_in_dim(w_first, dom_index * share, share, 0),
            lax.dynamic_slice_in_dim(w_second, dom_index * share, share, 0),
            bias_row,
        ],
        0,
    )
    along = lax.all_gather(payload, "fsdp", axis=0)
    sent_first = picked(history_first, chosen)
    sent_first, chosen = lax.optimization_barrier((sent_first, chosen))
    arrived_first = pull(sent_first)
    sent_second = picked(history_second, chosen)
    bias_full = along[:, 2 * share, : bias_first.shape[0]].reshape(hidden_width)
    both = lax.all_gather(along[:, : 2 * share], "dom", axis=0)
    both = both.reshape(dom_size, fsdp_size, 2, share, hidden_width)
    both = both.transpose(2, 1, 0, 3, 4).reshape(2, width, hidden_width)
    first_turned = both[0].T
    second_full = both[1]

    scalars = (tile_src, tile_count)
    wide = count * block
    mat = 2 * width * hidden_width * wide
    back_hidden = local_call(
        back_kernel,
        "back_to_hidden",
        scalars,
        (second_full, out_grad, tile_values),
        jax.ShapeDtypeStruct((count, hidden_width, block), F32),
        [
            pltpu.VMEM((hidden_width, wide), BF16),
            pltpu.VMEM((count, hidden_width, block), BF16),
        ],
        2 * mat,
    )
    sent_second, arrived_first = lax.optimization_barrier((sent_second, arrived_first))
    arrived_second = pull(sent_second)
    hidden_new, first_term, bias_rows = local_call(
        first_kernel,
        "first_layer",
        scalars,
        (
            features,
            arrived_first,
            tile_values,
            first_turned,
            bias_full.astype(F32)[:, None],
            back_hidden,
        ),
        (
            jax.ShapeDtypeStruct((count, hidden_width, block), BF16),
            jax.ShapeDtypeStruct((width, hidden_width), F32),
            jax.ShapeDtypeStruct((8, hidden_width), F32),
        ),
        [
            pltpu.VMEM((width, block), F32),
            pltpu.VMEM((width, wide), BF16),
            pltpu.VMEM((hidden_width, wide), BF16),
        ],
        4 * mat,
    )
    def near_sum(term, split, extra=None):
        terms = term.reshape(z_size, x_size, y_size, cores, share, hidden_width)
        terms = scatter_sum(terms, 3, core_hop, core, cores)
        if extra is not None:
            terms = jnp.concatenate([terms, extra], 3)
        if not split:
            terms = scatter_sum(terms, 1, x_hop, x, x_size)
            return scatter_sum(terms, 1, y_hop, y, y_size)
        cut = hidden_width // 2
        left = scatter_sum(terms[..., :cut], 1, x_hop, x, x_size)
        right = scatter_sum(terms[..., cut:], 2, y_hop, y, y_size)
        left = scatter_sum(left, 1, y_hop, y, y_size)
        right = scatter_sum(right, 1, x_hop, x, x_size)
        return jnp.concatenate([left, right], -1)

    bias_len = bias_first.shape[0]
    bias_share = bias_len // dom_size
    bias_terms = bias_rows[0].reshape(z_size, x_size, y_size, cores, 1, bias_share)
    bias_terms = scatter_sum(bias_terms, 3, core_hop, core, cores)
    bias_terms = jnp.pad(
        bias_terms, ((0, 0), (0, 0), (0, 0), (0, 7), (0, hidden_width - bias_share))
    )
    first_near = near_sum(first_term, False, bias_terms)
    hidden_held, arrived_second, first_near = lax.optimization_barrier(
        (hidden_new, arrived_second, first_near)
    )
    second_term = local_call(
        second_kernel,
        "second_layer",
        scalars,
        (hidden_held, arrived_second, tile_values, out_grad),
        jax.ShapeDtypeStruct((hidden_width, hidden_width), F32),
        [
            pltpu.VMEM((hidden_width, block), F32),
            pltpu.VMEM((hidden_width, wide), BF16),
            pltpu.VMEM((hidden_width, wide), BF16),
        ],
        3 * mat,
    )
    near = jnp.concatenate([first_near, near_sum(second_term, True)], 1)
    piece = scatter_sum(near, 0, z_hop, z, z_size).astype(BF16)
    pieces = gather_all(piece, y_hop, y, y_size)
    pieces = gather_all(pieces, core_hop, core, cores)
    pieces = pieces.transpose(1, 0, 2, 3).astype(F32)
    first_total = pieces[:, :, :share].reshape(rows, hidden_width)
    second_total = pieces[:, :, share + 8 :].reshape(rows, hidden_width)
    bias_total = pieces[:, :, share, :bias_share].reshape(bias_len)
    return (hidden_new, first_total, second_total, bias_total)


def solution(mesh):
    return jax.shard_map(
        on_device,
        mesh=mesh,
        in_specs=(
            P(("dom", "fsdp"), None, None),
            P("dom", "fsdp", None),
            P("dom", "fsdp", None),
            P("dom", None, None),
            P("dom", None),
            P(("dom", "fsdp"), None),
            P(("dom", "fsdp")),
            P(("dom", "fsdp"), None, None, None),
            P("fsdp", None),
            P("fsdp", None),
            P("fsdp"),
            P(("dom", "fsdp"), None, None),
        ),
        out_specs=(P(("dom", "fsdp"), None, None), P("fsdp", None), P("fsdp", None), P("fsdp")),
        check_vma=False,
    )
```
